256 devices in a mesh: replica: 8 (over y, x_hi), fsdp: 32 (over x_lo, z, core).
Axes of the slice: x: 4 (x_hi: 2, x_lo: 2; x = x_hi * 2 + x_lo), y: 4, z: 8, core: 2. Of those that a mesh axis runs over, the one named last changes fastest.
Arguments:
- hidden: bfloat16 [8, 16384, 4096], P('replica', 'fsdp'), may hold values from -6 to 6
- kv_weight: bfloat16 [8, 4096, 1024], P('replica', 'fsdp'), may hold values from -0.09375 to 0.09375
- kv_cotangent: bfloat16 [8, 16384, 1024], P('replica', 'fsdp'), may hold values from -6 to 6
- outer_global: float32 [4096, 512], P('fsdp'), may hold values from -6 to 6
- outer_local: float32 [8, 4096, 512], P('replica', 'fsdp'), may hold values from -6 to 6
- outer_momentum: float32 [4096, 512], P('fsdp'), may hold values from -6 to 6
Outputs:
- kv_out: bfloat16 [8, 16384, 1024], P('replica', 'fsdp')
- grad_hidden: bfloat16 [8, 16384, 4096], P('replica', 'fsdp')
- grad_weight: float32 [8, 4096, 1024], P('replica', 'fsdp')
- new_global: float32 [4096, 512], P('fsdp')
- new_momentum: float32 [4096, 512], P('fsdp')
The draws below stay inside these ranges and needn't reach their ends.
All inputs are finite; a program needn't handle non-finite values.
Results may differ from the reference program's by a relative error of at most 0.001.
Values may be sent and summed in bfloat16 or wider, within the bound.
No kernel may reach another device: no remote copies, remote signals or barrier semaphores. Data moves between devices by JAX's collectives and lax.ppermute only.
A program may use at most 128 MiB of HBM per device.

```python
import jax
import jax.numpy as jnp
from jax import lax

D = 4096
KVW = 1024
OW = 512
TOKENS_REP = 16384
REPLICAS = 8


def strengthened(result, rng, source, target, blocks, factor):
    def block_of(axis_at):
        return (jnp.arange(result.shape[axis_at]) // (result.shape[axis_at] // blocks)).reshape((-1,) + (1,) * (result.ndim - 1 - axis_at))

    near = jax.random.permutation(rng, blocks)[block_of(target)]
    far = (block_of(target) + blocks // 2) % blocks
    return jnp.where((block_of(source) == near) | (block_of(source) == far), factor * result, result)


def steps_of(own_key, shape, split, smallest, high):
    def one(dim, blocks):
        heights = jax.random.uniform(jax.random.fold_in(jax.random.fold_in(own_key, 6), dim), (blocks,), jnp.float32, smallest / len(split), high / len(split))
        return jnp.repeat(jnp.exp(heights), shape[dim] // blocks).reshape((-1,) + (1,) * (len(shape) - dim - 1))

    level = one(*split[0])
    for cut in split[1:]:
        level = level * one(*cut)
    return level


def noise(stream_key, shape, spread, most, shards=(), held_as=jnp.bfloat16):
    values = spread * jax.random.normal(stream_key, shape, jnp.float32)
    if shards:
        values = values * steps_of(stream_key, shape, shards, -0.22, 0.18)
    return jnp.clip(values, -most, most).astype(held_as)


def gaussian_with(key, shape, scale, reach, split, heavy, dtype=jnp.bfloat16):
    result = scale * jax.random.normal(key, shape, jnp.float32)
    if split:
        result = result * steps_of(key, shape, split, -0.22, 0.18)
    return jnp.clip(strengthened(result, jax.random.fold_in(key, 3), *heavy), -reach, reach).astype(dtype)


def setup_inputs(seed: int = 0) -> dict:
    streams_of = jax.random.split(jax.random.key(seed), 7)
    return {
        "hidden": gaussian_with(streams_of[0], (REPLICAS, TOKENS_REP, D), 1.0, 6.0, ((0, 8), (1, 32)), (1, 2, 32, 2.75)),
        "kv_weight": noise(streams_of[1], (REPLICAS, D, KVW), D ** -0.5, 0.09375, ((0, 8), (1, 32))),
        "kv_cotangent": noise(streams_of[2], (REPLICAS, TOKENS_REP, KVW), 1.0, 6.0, ((0, 8), (1, 32))),
        "outer_global": noise(streams_of[3], (D, OW), 1.0, 6.0, ((0, 32),), jnp.float32),
        "outer_local": noise(streams_of[4], (REPLICAS, D, OW), 1.0, 6.0, ((0, 8), (1, 32)), jnp.float32),
        "outer_momentum": noise(streams_of[5], (D, OW), 1.0, 6.0, ((0, 32),), jnp.float32),
    }


def reference(hidden, kv_weight, kv_cotangent, outer_global, outer_local, outer_momentum):
    scale = TOKENS_REP ** -0.5

    def one_replica(items):
        rows, weight, cot = items
        keys = jnp.dot(rows, weight, preferred_element_type=jnp.float32).astype(jnp.bfloat16)
        back = lax.dot_general(cot, weight, (((1,), (1,)), ((), ())), preferred_element_type=jnp.float32).astype(jnp.bfloat16)
        grads = lax.dot_general(rows, cot, (((0,), (0,)), ((), ())), preferred_element_type=jnp.float32) * scale
        return keys, back, grads

    kv_out, grad_hidden, grad_weight = lax.map(one_replica, (hidden, kv_weight, kv_cotangent))
    outer_grad = jnp.sum(outer_global[None] - outer_local, axis=0) / REPLICAS
    new_momentum = 0.9 * outer_momentum + outer_grad
    new_global = outer_global - 0.7 * (outer_grad + 0.9 * new_momentum)
    return kv_out, grad_hidden, grad_weight, new_global, new_momentum
```

```python
import functools

import jax
import jax.numpy as jnp
from jax import lax
from jax.experimental import pallas as pl
from jax.experimental.pallas import tpu as pltpu
from jax.sharding import PartitionSpec as P

BF16, F16, F32 = jnp.bfloat16, jnp.float16, jnp.float32
ZS, CORES, XS = 8, 2, 2
UP = 8.0
ORDER = (4, 3, -3, 2, -2, 1, -1, 0)
VMEM = 60 * 1024 * 1024


def fsdp_perm(fn):
    pairs = []
    for x in range(XS):
        for z in range(ZS):
            for c in range(CORES):
                nx, nz, nc = fn(x, z, c)
                pairs.append((x * 16 + z * 2 + c, nx * 16 + (nz % ZS) * 2 + nc))
    return pairs


Z_UP = fsdp_perm(lambda x, z, c: (x, z + 1, c))
Z_DOWN = fsdp_perm(lambda x, z, c: (x, z - 1, c))
X_SWAP = fsdp_perm(lambda x, z, c: (1 - x, z, c))
CORE_SWAP = fsdp_perm(lambda x, z, c: (x, z, 1 - c))


def send(value, pairs):
    return lax.ppermute(value, "fsdp", pairs)


def params():
    return pltpu.CompilerParams(vmem_limit_bytes=VMEM)


def pack_kernel(index, src, dst):
    dst[...] = src[...]


def pack(hidden, index):
    tokens = hidden.shape[0]
    count = index.shape[0]
    return pl.pallas_call(
        pack_kernel,
        out_shape=jax.ShapeDtypeStruct((tokens, count * 128), hidden.dtype),
        grid_spec=pltpu.PrefetchScalarGridSpec(
            num_scalar_prefetch=1,
            grid=(count,),
            in_specs=[pl.BlockSpec((tokens, 128), lambda i, index: (0, index[i]))],
            out_specs=pl.BlockSpec((tokens, 128), lambda i, index: (0, i)),
        ),
        name="pack",
    )(index, hidden)


def grad_kernel(sizes, scale, index, *refs):
    count = len(ORDER)
    own = jnp.concatenate([r[...] for r in refs[:count]], axis=1)
    other_rows, own_cot, other_cot = refs[count : count + 3]
    outs = refs[count + 3 :]
    dims = (((0,), (0,)), ((), ()))
    width = own_cot.shape[1]
    step = 512
    for n in range(0, width, step):
        cols = slice(n, n + step)
        total = lax.dot_general(own, own_cot[:, cols], dims, preferred_element_type=F32)
        total += lax.dot_general(other_rows[...], other_cot[:, cols], dims, preferred_element_type=F32)
        total = total * scale
        at = 0
        for out, size in zip(outs, sizes):
            out[:, cols] = total[at : at + size].astype(out.dtype)
            at += size


def grad(hidden, index, other_rows, cot, other_cot, sizes, dtype, scale):
    tokens, width = cot.shape
    count = len(ORDER)

    def block(k):
        return pl.BlockSpec((tokens, 128), lambda i, index: (0, index[k]))

    def whole(shape):
        return pl.BlockSpec(shape, lambda i, index: (0, 0))

    flops = 2 * 2 * tokens * count * 128 * width
    return pl.pallas_call(
        functools.partial(grad_kernel, sizes, scale),
        out_shape=[jax.ShapeDtypeStruct((s, width), dtype) for s in sizes],
        grid_spec=pltpu.PrefetchScalarGridSpec(
            num_scalar_prefetch=1,
            grid=(1,),
            in_specs=[block(k) for k in range(count)]
            + [whole((tokens, count * 128)), whole((tokens, width)), whole((tokens, width))],
            out_specs=[whole((s, width)) for s in sizes],
        ),
        compiler_params=params(),
        cost_estimate=pl.CostEstimate(flops=flops, bytes_accessed=8 << 20, transcendentals=0),
        name="grad",
    )(index, *([hidden] * count), other_rows, cot, other_cot)


def use_kernel(count, first, last, index, *refs):
    rows = jnp.concatenate([r[...] for r in refs[:count]], axis=1)
    weight = jnp.concatenate([r[...] for r in refs[count : 2 * count]], axis=0)
    refs = refs[2 * count :]
    cot, refs = refs[0], refs[1:]
    if not first:
        acc, _, refs = refs[0], refs[1], refs[2:]
    out_keys, out_back, block, sems = refs
    block[...] = lax.dot_general(
        cot[...], weight, (((1,), (1,)), ((), ())), preferred_element_type=F32
    ).astype(BF16)
    copies = []
    for k in range(count):
        copies.append(
            pltpu.make_async_copy(
                block.at[:, pl.ds(k * 128, 128)],
                out_back.at[:, pl.ds(pl.multiple_of(index[k] * 128, 128), 128)],
                sems.at[k],
            )
        )
        copies[-1].start()
    keys = jnp.dot(rows, weight, preferred_element_type=F32)
    if not first:
        keys += acc[...]
    out_keys[...] = keys.astype(out_keys.dtype)
    for copy in copies:
        copy.wait()


def use(hidden, cot, index, weights, state, last):
    tokens, width = cot.shape
    count = len(weights)
    first = state is None

    def block(k):
        return pl.BlockSpec((tokens, 128), lambda i, index: (0, index[k]))

    def whole(shape):
        return pl.BlockSpec(shape, lambda i, index: (0, 0))

    anywhere = pl.BlockSpec(memory_space=pl.ANY)
    in_specs = [block(k) for k in range(count)] + [whole((128, width))] * count + [whole((tokens, width))]
    operands = [hidden] * count + list(weights) + [cot]
    aliases = {}
    if not first:
        in_specs += [whole((tokens, width)), anywhere]
        operands += list(state)
        aliases = {2 * count + 3: 1}
    flops = 2 * 2 * tokens * count * 128 * width
    return pl.pallas_call(
        functools.partial(use_kernel, count, first, last),
        out_shape=[
            jax.ShapeDtypeStruct((tokens, width), BF16 if last else F32),
            jax.ShapeDtypeStruct(hidden.shape, BF16),
        ],
        grid_spec=pltpu.PrefetchScalarGridSpec(
            num_scalar_prefetch=1,
            grid=(1,),
            in_specs=in_specs,
            out_specs=[whole((tokens, width)), anywhere],
            scratch_shapes=[
                pltpu.VMEM((tokens, count * 128), BF16),
                pltpu.SemaphoreType.DMA((count,)),
            ],
        ),
        input_output_aliases=aliases,
        compiler_params=params(),
        cost_estimate=pl.CostEstimate(flops=flops, bytes_accessed=6 << 20, transcendentals=0),
        name="use",
    )(index, *operands)


def outer_update(global_rows, momentum_rows, outer_grad):
    new_momentum = 0.9 * momentum_rows + outer_grad
    new_global = global_rows - 0.7 * (outer_grad + 0.9 * new_momentum)
    return (new_global, new_momentum)


def local(hidden, kv_weight, kv_cotangent, outer_global, outer_local, outer_momentum):
    rows = hidden[0]
    cot = kv_cotangent[0]
    shard = kv_weight[0]
    scale = (rows.shape[0] * lax.axis_size("fsdp")) ** (-0.5)
    me = lax.axis_index("fsdp")
    x, z, c = me // 16, (me // 2) % ZS, me % 2

    def where(dx, dz, dc):
        return ((x + dx) % 2) * 16 + ((z + dz) % ZS) * 2 + (c + dc) % 2

    def blocks(dx, dc):
        return jnp.stack([where(dx, dz, dc) for dz in ORDER]).astype(jnp.int32)

    a_up, a_down = {0: shard}, {0: shard}
    a_up[1], a_down[1] = send(shard, Z_UP), send(shard, Z_DOWN)
    b0 = send(shard, X_SWAP)
    b_up, b_down = {0: b0}, {0: b0}

    other_cot = send(cot, CORE_SWAP)
    far_other = send(pack(rows, blocks(1, 1)), CORE_SWAP)
    near_other = send(pack(rows, blocks(0, 1)), CORE_SWAP)

    b_up[1], b_down[1] = send(b0, Z_UP), send(b0, Z_DOWN)

    sizes = (128, 256, 256, 384)
    far = grad(rows, blocks(1, 0), far_other, cot, other_cot, sizes, F32, scale * UP)
    came = [send(f.astype(F16), X_SWAP) for f in far]
    near = grad(rows, blocks(0, 0), near_other, cot, other_cot, sizes, F32, scale * UP)
    both = [n + f.astype(F32) for n, f in zip(near, came)]
    by = {4: both[0], 3: both[1][:128], -3: both[1][128:], 2: both[2][:128], -2: both[2][128:]}
    by.update({1: both[3][:128], -1: both[3][128:256], 0: both[3][256:]})

    for hop in (2, 3):
        a_up[hop], a_down[hop] = send(a_up[hop - 1], Z_UP), send(a_down[hop - 1], Z_DOWN)
        b_up[hop], b_down[hop] = send(b_up[hop - 1], Z_UP), send(b_down[hop - 1], Z_DOWN)
    a_up[4] = send(a_up[3], Z_UP)
    b_down[4] = send(b_down[3], Z_DOWN)

    pieces = {0: [(0, 0, shard), (1, 0, b0)]}
    for hop in (1, 2, 3):
        pieces[hop] = [(0, -hop, a_up[hop]), (0, hop, a_down[hop]), (1, -hop, b_up[hop]), (1, hop, b_down[hop])]
    pieces[4] = [(0, 4, a_up[4]), (1, 4, b_down[4])]
    state = None
    for hops in ((0, 1), (2, 3), (4,)):
        weights, index = [], []
        for hop in hops:
            for dx, dz, w in pieces[hop]:
                weights += [w, send(w, CORE_SWAP)]
                index += [where(dx, dz, 0), where(dx, dz, 1)]
        state = use(rows, cot, jnp.stack(index).astype(jnp.int32), weights, state, hops == (4,))
    keys, back = state

    half = 64
    up = send(by[4][:half].astype(F16), Z_UP)
    down = send(by[4][half:].astype(F16), Z_DOWN)
    for hop in (3, 2, 1):
        if hop == 3:
            up = jnp.concatenate([by[3][:half] + up.astype(F32), by[3][half:]], axis=0)
            down = jnp.concatenate([by[-3][:half], by[-3][half:] + down.astype(F32)], axis=0)
        else:
            up = by[hop] + up.astype(F32)
            down = by[-hop] + down.astype(F32)
        up, down = send(up.astype(F16), Z_UP), send(down.astype(F16), Z_DOWN)
    grads = (by[0] + up.astype(F32) + down.astype(F32)) * (1.0 / UP)

    replica_count = lax.axis_size("replica")
    total = outer_global - outer_local[0]
    for bit in (1, 2, 4):
        total = total + lax.ppermute(total, "replica", [(r, r ^ bit) for r in range(replica_count)])
    new_global, new_momentum = outer_update(outer_global, outer_momentum, total / replica_count)
    return (keys[None], back[None], grads[None], new_global, new_momentum)


def solution(mesh):
    return jax.shard_map(
        local,
        mesh=mesh,
        in_specs=(
            P("replica", "fsdp", None),
            P("replica", "fsdp", None),
            P("replica", "fsdp", None),
            P("fsdp", None),
            P("replica", "fsdp", None),
            P("fsdp", None),
        ),
        out_specs=(
            P("replica", "fsdp", None),
            P("replica", "fsdp", None),
            P("replica", "fsdp", None),
            P("fsdp", None),
            P("fsdp", None),
        ),
        check_vma=False,
    )
```

```python
import functools

import jax
import jax.numpy as jnp
from jax import lax
from jax.experimental import pallas as pl
from jax.experimental.pallas import tpu as pltpu
from jax.sharding import PartitionSpec as P

BF16, F16, F32 = jnp.bfloat16, jnp.float16, jnp.float32
ZS, CORES, XS = 8, 2, 2
UP = 8.0
ORDER = (4, -3, 0, 3, -2, 2, -1, 1)


def fsdp_perm(fn):
    pairs = []
    for x in range(XS):
        for z in range(ZS):
            for c in range(CORES):
                nx, nz, nc = fn(x, z, c)
                pairs.append((x * 16 + z * 2 + c, nx * 16 + (nz % ZS) * 2 + nc))
    return pairs


Z_UP = fsdp_perm(lambda x, z, c: (x, z + 1 - 2 * c, c))
Z_DOWN = fsdp_perm(lambda x, z, c: (x, z - 1 + 2 * c, c))
X_SWAP = fsdp_perm(lambda x, z, c: (1 - x, z, c))
CORE_SWAP = fsdp_perm(lambda x, z, c: (x, z, 1 - c))


class Order:
    def __init__(self, place):
        self.place = place

    def wait(self, *values):
        *values, self.place = lax.optimization_barrier((*values, self.place))
        return values

    def gate(self, value):
        return lax.optimization_barrier((value, self.place))[0]


def block_at(place, dx, dz, dc):
    core = (place[2] + dc) % CORES
    return ((place[0] + dx) % XS) * 16 + ((place[1] + (1 - 2 * core) * dz + ZS) % ZS) * 2 + core


def columns(tokens, spot):
    return pl.BlockSpec(
        (tokens, 128), lambda i, place: (0, block_at(place, *spot)), pipeline_mode=pl.Buffered(1)
    )


def packed(tokens, k):
    return pl.BlockSpec((tokens, 128), lambda i, place: (0, k), pipeline_mode=pl.Buffered(1))


def whole(shape):
    return pl.BlockSpec(shape, lambda i, place: (0, 0), pipeline_mode=pl.Buffered(1))


def params(mib):
    return pltpu.CompilerParams(vmem_limit_bytes=mib << 20)


COST = pl.CostEstimate(flops=1 << 20, bytes_accessed=1 << 16, transcendentals=0)


def pack_kernel(place, *refs):
    count = len(ORDER)
    for half, out in enumerate(refs[2 * count :]):
        for k in range(count):
            out[:, k * 128 : (k + 1) * 128] = refs[half * count + k][...]


def pack(hidden, place):
    tokens = hidden.shape[0]
    count = len(ORDER)
    spots = [(dx, dz, 0) for dx in (0, 1) for dz in ORDER]
    shape = (tokens, count * 128)
    return pl.pallas_call(
        pack_kernel,
        out_shape=[jax.ShapeDtypeStruct(shape, hidden.dtype)] * 2,
        grid_spec=pltpu.PrefetchScalarGridSpec(
            num_scalar_prefetch=1,
            grid=(1,),
            in_specs=[columns(tokens, s) for s in spots],
            out_specs=[whole(shape)] * 2,
        ),
        compiler_params=params(8),
        cost_estimate=COST,
        name="pack",
    )(place, *([hidden] * len(spots)))


def grad_kernel(sizes, scale, place, *refs):
    count = len(ORDER)
    own = refs[0][...]
    other = jnp.concatenate([r[...] for r in refs[1 : count + 1]], axis=1)
    own_cot, other_cot = refs[count + 1 : count + 3]
    outs = refs[count + 3 :]
    dims = (((0,), (0,)), ((), ()))
    width = own_cot.shape[1]
    step = 512
    for n in range(0, width, step):
        cols = slice(n, n + step)
        total = lax.dot_general(own, own_cot[:, cols], dims, preferred_element_type=F32)
        total += lax.dot_general(other, other_cot[:, cols], dims, preferred_element_type=F32)
        total = total * scale
        at = 0
        for out, size in zip(outs, sizes):
            out[:, cols] = total[at : at + size].astype(out.dtype)
            at += size


def grad(place, dx, hidden, cot, sizes, scale):
    tokens, width = cot[0].shape
    count = len(ORDER)
    spots = [(dx, dz, 0) for dz in ORDER]
    return pl.pallas_call(
        functools.partial(grad_kernel, sizes, scale),
        out_shape=[jax.ShapeDtypeStruct((s, width), F32) for s in sizes],
        grid_spec=pltpu.PrefetchScalarGridSpec(
            num_scalar_prefetch=1,
            grid=(1,),
            in_specs=[whole((tokens, count * 128))]
            + [columns(tokens, s) for s in spots]
            + [whole((tokens, width))] * 2,
            out_specs=[whole((s, width)) for s in sizes],
        ),
        compiler_params=params(24),
        cost_estimate=COST,
        name="grad",
    )(place, hidden[0][dx], *([hidden[1]] * count), *cot)


def use_kernel(spots, arrays, first, place, *refs):
    count = len(spots)
    rows = [jnp.concatenate([r[...] for r in refs[k * count : (k + 1) * count]], axis=1) for k in range(2)]
    refs = refs[2 * count :]
    weight = jnp.concatenate([r[...] for r in refs[:arrays]], axis=0)
    refs = refs[arrays:]
    cot, refs = refs[:2], refs[2:]
    if not first:
        acc, refs = refs[:2], refs[3:]
    out_keys, out_back, out_other, block, sems = refs[:2], refs[2], refs[3], refs[4], refs[5]
    dims = (((1,), (1,)), ((), ()))
    block[...] = lax.dot_general(cot[0][...], weight, dims, preferred_element_type=F32).astype(BF16)
    copies = []
    for k, spot in enumerate(spots):
        at = pl.multiple_of(block_at(place, *spot) * 128, 128)
        copies.append(
            pltpu.make_async_copy(
                block.at[:, pl.ds(k * 128, 128)], out_back.at[:, pl.ds(at, 128)], sems.at[k]
            )
        )
        copies[-1].start()
    out_other[...] = lax.dot_general(cot[1][...], weight, dims, preferred_element_type=F32).astype(BF16)
    for k in range(2):
        keys = jnp.dot(rows[k], weight, preferred_element_type=F32)
        if not first:
            keys += acc[k][...]
        out_keys[k][...] = keys
    for copy in copies:
        copy.wait()


def use(place, hidden, cot, weights, spots, state, last=False):
    tokens, width = cot[0].shape
    count = len(spots)
    first = state is None
    flops = 8 * tokens * count * 128 * width
    cost = pl.CostEstimate(flops=flops, bytes_accessed=1 << 20, transcendentals=0)
    anywhere = pl.BlockSpec(memory_space=pl.ANY)
    in_specs = [packed(tokens, ORDER.index(s[1])) for s in spots] + [columns(tokens, s) for s in spots]
    in_specs += [whole(w.shape) for w in weights] + [whole((tokens, width))] * 2
    operands = [hidden[0][s[0]] for s in spots] + [hidden[1]] * count + list(weights) + list(cot)
    aliases = {}
    if not first:
        in_specs += [whole((tokens, width))] * 2 + [anywhere]
        operands += list(state)
        aliases = {len(operands): 2}
    return pl.pallas_call(
        functools.partial(use_kernel, spots, len(weights), first),
        out_shape=[
            jax.ShapeDtypeStruct((tokens, width), F32),
            jax.ShapeDtypeStruct((tokens, width), F32),
            jax.ShapeDtypeStruct(hidden[1].shape, BF16),
            jax.ShapeDtypeStruct((tokens, count * 128), BF16),
        ],
        grid_spec=pltpu.PrefetchScalarGridSpec(
            num_scalar_prefetch=1,
            grid=(1,),
            in_specs=in_specs,
            out_specs=[whole((tokens, width))] * 2 + [anywhere, whole((tokens, count * 128))],
            scratch_shapes=[
                pltpu.VMEM((tokens, count * 128), BF16),
                pltpu.SemaphoreType.DMA((count,)),
            ],
        ),
        input_output_aliases=aliases,
        compiler_params=params(40),
        cost_estimate=COST if last else cost,
        name="use",
    )(place, *operands)


def merge_kernel(groups, place, *refs):
    parts, out, sems = refs[: len(groups)], refs[len(groups) + 1], refs[len(groups) + 2]
    copies = []
    for part, spots in zip(parts, groups):
        for k, (dx, dz, _) in enumerate(spots):
            at = pl.multiple_of(block_at(place, dx, dz, 1) * 128, 128)
            copies.append(
                pltpu.make_async_copy(
                    part.at[:, pl.ds(k * 128, 128)], out.at[:, pl.ds(at, 128)], sems.at[len(copies)]
                )
            )
            copies[-1].start()
    for copy in copies:
        copy.wait()


def merge(place, parts, groups, back):
    anywhere = pl.BlockSpec(memory_space=pl.ANY)
    return pl.pallas_call(
        functools.partial(merge_kernel, groups),
        out_shape=jax.ShapeDtypeStruct(back.shape, back.dtype),
        grid_spec=pltpu.PrefetchScalarGridSpec(
            num_scalar_prefetch=1,
            grid=(1,),
            in_specs=[whole(p.shape) for p in parts] + [anywhere],
            out_specs=anywhere,
            scratch_shapes=[pltpu.SemaphoreType.DMA((sum(map(len, groups)),))],
        ),
        input_output_aliases={len(parts) + 1: 0},
        compiler_params=params(16),
        cost_estimate=COST,
        name="merge",
    )(place, *parts, back)


def outer_update(global_rows, momentum_rows, outer_grad):
    new_momentum = 0.9 * momentum_rows + outer_grad
    new_global = global_rows - 0.7 * (outer_grad + 0.9 * new_momentum)
    return (new_global, new_momentum)


def local(hidden, kv_weight, kv_cotangent, outer_global, outer_local, outer_momentum):
    rows = hidden[0]
    cot = kv_cotangent[0]
    shard = kv_weight[0]
    scale = (rows.shape[0] * lax.axis_size("fsdp")) ** (-0.5)
    me = lax.axis_index("fsdp")
    place = jnp.stack([me // 16, (me // 2) % ZS, me % 2]).astype(jnp.int32)
    step = Order(place)
    replica_count = lax.axis_size("replica")

    def send(value, pairs):
        return lax.ppermute(step.gate(value), "fsdp", pairs)

    def butterfly(value, bit):
        pairs = [(r, r ^ bit) for r in range(replica_count)]
        return lax.ppermute(step.gate(value), "replica", pairs)

    def both_ways(above, below):
        above, below = step.wait(above.astype(F16), below.astype(F16))
        return send(above, Z_UP), send(below, Z_DOWN)

    b0 = send(shard, X_SWAP)
    other = send(rows, CORE_SWAP), send(cot, CORE_SWAP)
    total = outer_global - outer_local[0]
    summed = butterfly(total, 2)
    own = pack(rows, step.place)
    b0, summed, *both = step.wait(b0, summed, *other, *own)
    total = total + summed
    hidden2, cot2 = (both[2:], both[0]), (cot, both[1])
    pair = jnp.concatenate([shard, b0], axis=0)
    up1, down1 = send(pair, Z_UP), send(pair, Z_DOWN)
    summed = butterfly(total, 4)

    sizes = (384, 256, 256, 128)
    far = grad(step.place, 1, hidden2, cot2, sizes, scale * UP)
    far = step.wait(*[f.astype(F16) for f in far])
    got_a, got_b = send(far[0], X_SWAP), send(far[1], X_SWAP)
    near = step.wait(*grad(step.place, 0, hidden2, cot2, sizes, scale * UP))

    up1, down1, summed = step.wait(up1, down1, summed)
    total = total + summed
    up2, down2 = send(up1, Z_UP), send(down1, Z_DOWN)
    spots = [(0, 0, 0), (1, 0, 0), (0, -1, 0), (1, -1, 0), (0, 1, 0), (1, 1, 0)]
    groups = [spots]
    *state, back1 = step.wait(*use(step.place, hidden2, cot2, [pair, up1, down1], spots, None))

    (got,) = step.wait(got_a)
    both = near[0] + got.astype(F32)
    above, below = send(both[:128].astype(F16), Z_UP), send(both[128:256].astype(F16), Z_DOWN)
    mine = both[256:]
    up2, down2 = step.wait(up2, down2)
    up3, down3 = send(up2, Z_UP), send(down2, Z_DOWN)

    above, below, got = step.wait(above, below, got_b)
    both = near[1] + got.astype(F32)
    above, below = both[:128] + above.astype(F32), both[128:] + below.astype(F32)
    above, below = send(above.astype(F16), Z_UP), send(below.astype(F16), Z_DOWN)
    got = send(far[2], X_SWAP)
    spots = [(0, -2, 0), (1, -2, 0), (0, 2, 0), (1, 2, 0)]
    groups.append(spots)
    *state, back2 = step.wait(*use(step.place, hidden2, cot2, [up2, down2], spots, state))

    up3, down3 = step.wait(up3, down3)
    up4, down4 = send(up3[:128], Z_UP), send(down3[128:], Z_DOWN)
    above, below, got = step.wait(above, below, got)
    both = near[2] + got.astype(F32)
    above, below = both[:128] + above.astype(F32), both[128:] + below.astype(F32)
    above, below = send(above.astype(F16), Z_UP), send(below.astype(F16), Z_DOWN)
    got = send(far[3], X_SWAP)
    spots = [(0, -3, 0), (1, -3, 0), (0, 3, 0), (1, 3, 0)]
    groups.append(spots)
    *state, back3 = step.wait(*use(step.place, hidden2, cot2, [up3, down3], spots, state, True))
    up4, down4 = step.wait(up4, down4)
    spots = [(0, 4, 0), (1, 4, 0)]
    groups.append(spots)
    keys, other_keys, back, back4 = step.wait(*use(step.place, hidden2, cot2, [up4, down4], spots, state, True))

    above, below, got = step.wait(above, below, got)
    both = near[3] + got.astype(F32)
    mine = mine + below.astype(F32)
    above = send((both + above.astype(F32)).astype(F16), Z_UP)
    summed = butterfly(total, 1)
    other_keys = send(other_keys, CORE_SWAP)
    back1 = send(jnp.concatenate([back1, back2], axis=1), CORE_SWAP)
    back3 = send(jnp.concatenate([back3, back4], axis=1), CORE_SWAP)
    other_keys, back1, back3 = step.wait(other_keys, back1, back3)
    back = merge(step.place, [back1, back3], [groups[0] + groups[1], groups[2] + groups[3]], back)
    keys = (keys + other_keys).astype(BF16)
    keys, back, summed = step.wait(keys, back, summed)
    new_global, new_momentum = outer_update(outer_global, outer_momentum, (total + summed) / replica_count)
    above, keys, back, new_global, new_momentum = step.wait(above, keys, back, new_global, new_momentum)
    grads = (mine + above.astype(F32)) * (1.0 / UP)
    return (keys[None], back[None], grads[None], new_global, new_momentum)


def solution(mesh):
    return jax.shard_map(
        local,
        mesh=mesh,
        in_specs=(
            P("replica", "fsdp", None),
            P("replica", "fsdp", None),
            P("replica", "fsdp", None),
            P("fsdp", None),
            P("replica", "fsdp", None),
            P("fsdp", None),
        ),
        out_specs=(
            P("replica", "fsdp", None),
            P("replica", "fsdp", None),
            P("replica", "fsdp", None),
            P("fsdp", None),
            P("fsdp", None),
        ),
        check_vma=False,
    )
```

```python
import functools

import jax
import jax.numpy as jnp
from jax import lax
from jax.experimental import pallas as pl
from jax.experimental.pallas import tpu as pltpu
from jax.sharding import PartitionSpec as P

BF16, F16, F32 = jnp.bfloat16, jnp.float16, jnp.float32
ZS, CORES, XS = 8, 2, 2
UP = 8.0
ORDER = (4, -3, 0, 3, -2, 2, -1, 1)


def fsdp_perm(fn):
    pairs = []
    for x in range(XS):
        for z in range(ZS):
            for c in range(CORES):
                nx, nz, nc = fn(x, z, c)
                pairs.append((x * 16 + z * 2 + c, nx * 16 + (nz % ZS) * 2 + nc))
    return pairs


Z_UP = fsdp_perm(lambda x, z, c: (x, z + 1 - 2 * c, c))
Z_DOWN = fsdp_perm(lambda x, z, c: (x, z - 1 + 2 * c, c))
X_SWAP = fsdp_perm(lambda x, z, c: (1 - x, z, c))
CORE_SWAP = fsdp_perm(lambda x, z, c: (x, z, 1 - c))


class Order:
    def __init__(self, place):
        self.place = place

    def wait(self, *values):
        *values, self.place = lax.optimization_barrier((*values, self.place))
        return values

    def gate(self, value):
        return lax.optimization_barrier((value, self.place))[0]


def block_at(place, dx, dz, dc):
    core = (place[2] + dc) % CORES
    return ((place[0] + dx) % XS) * 16 + ((place[1] + (1 - 2 * core) * dz + ZS) % ZS) * 2 + core


def columns(tokens, spot):
    return pl.BlockSpec(
        (tokens, 128), lambda i, place: (0, block_at(place, *spot)), pipeline_mode=pl.Buffered(1)
    )


def packed(tokens, k):
    return pl.BlockSpec((tokens, 128), lambda i, place: (0, k), pipeline_mode=pl.Buffered(1))


def whole(shape):
    return pl.BlockSpec(shape, lambda i, place: (0, 0), pipeline_mode=pl.Buffered(1))


def params(mib):
    return pltpu.CompilerParams(vmem_limit_bytes=mib << 20)


COST = pl.CostEstimate(flops=1 << 20, bytes_accessed=1 << 16, transcendentals=0)


def pack_kernel(place, *refs):
    count = len(ORDER)
    for half, out in enumerate(refs[2 * count :]):
        for k in range(count):
            out[:, k * 128 : (k + 1) * 128] = refs[half * count + k][...]


def pack(hidden, place):
    tokens = hidden.shape[0]
    count = len(ORDER)
    spots = [(dx, dz, 0) for dx in (0, 1) for dz in ORDER]
    shape = (tokens, count * 128)
    return pl.pallas_call(
        pack_kernel,
        out_shape=[jax.ShapeDtypeStruct(shape, hidden.dtype)] * 2,
        grid_spec=pltpu.PrefetchScalarGridSpec(
            num_scalar_prefetch=1,
            grid=(1,),
            in_specs=[columns(tokens, s) for s in spots],
            out_specs=[whole(shape)] * 2,
        ),
        compiler_params=params(8),
        cost_estimate=COST,
        name="pack",
    )(place, *([hidden] * len(spots)))


def grad_kernel(sizes, scale, place, *refs):
    count = len(ORDER)
    own = refs[0][...]
    other = jnp.concatenate([r[...] for r in refs[1 : count + 1]], axis=1)
    own_cot, other_cot = refs[count + 1 : count + 3]
    outs = refs[count + 3 :]
    dims = (((0,), (0,)), ((), ()))
    width = own_cot.shape[1]
    step = 512
    for n in range(0, width, step):
        cols = slice(n, n + step)
        total = lax.dot_general(own, own_cot[:, cols], dims, preferred_element_type=F32)
        total += lax.dot_general(other, other_cot[:, cols], dims, preferred_element_type=F32)
        total = total * scale
        at = 0
        for out, size in zip(outs, sizes):
            out[:, cols] = total[at : at + size].astype(out.dtype)
            at += size


def grad(place, dx, hidden, cot, sizes, scale):
    tokens, width = cot[0].shape
    count = len(ORDER)
    spots = [(dx, dz, 0) for dz in ORDER]
    return pl.pallas_call(
        functools.partial(grad_kernel, sizes, scale),
        out_shape=[jax.ShapeDtypeStruct((s, width), F32) for s in sizes],
        grid_spec=pltpu.PrefetchScalarGridSpec(
            num_scalar_prefetch=1,
            grid=(1,),
            in_specs=[whole((tokens, count * 128))]
            + [columns(tokens, s) for s in spots]
            + [whole((tokens, width))] * 2,
            out_specs=[whole((s, width)) for s in sizes],
        ),
        compiler_params=params(24),
        cost_estimate=COST,
        name="grad",
    )(place, hidden[0][dx], *([hidden[1]] * count), *cot)


def use_kernel(spots, arrays, first, place, *refs):
    count = len(spots)
    rows = [jnp.concatenate([r[...] for r in refs[k * count : (k + 1) * count]], axis=1) for k in range(2)]
    refs = refs[2 * count :]
    weight = jnp.concatenate([r[...] for r in refs[:arrays]], axis=0)
    refs = refs[arrays:]
    cot, refs = refs[:2], refs[2:]
    if not first:
        acc, refs = refs[:2], refs[3:]
    out_keys, out_back, out_other, block, sems = refs[:2], refs[2], refs[3], refs[4], refs[5]
    dims = (((1,), (1,)), ((), ()))
    block[...] = lax.dot_general(cot[0][...], weight, dims, preferred_element_type=F32).astype(BF16)
    copies = []
    for k, spot in enumerate(spots):
        at = pl.multiple_of(block_at(place, *spot) * 128, 128)
        copies.append(
            pltpu.make_async_copy(
                block.at[:, pl.ds(k * 128, 128)], out_back.at[:, pl.ds(at, 128)], sems.at[k]
            )
        )
        copies[-1].start()
    out_other[...] = lax.dot_general(cot[1][...], weight, dims, preferred_element_type=F32).astype(BF16)
    for k in range(2):
        keys = jnp.dot(rows[k], weight, preferred_element_type=F32)
        if not first:
            keys += acc[k][...]
        out_keys[k][...] = keys
    for copy in copies:
        copy.wait()


def use(place, hidden, cot, weights, spots, state, last=False):
    tokens, width = cot[0].shape
    count = len(spots)
    first = state is None
    flops = 8 * tokens * count * 128 * width
    cost = pl.CostEstimate(flops=flops, bytes_accessed=1 << 20, transcendentals=0)
    anywhere = pl.BlockSpec(memory_space=pl.ANY)
    in_specs = [packed(tokens, ORDER.index(s[1])) for s in spots] + [columns(tokens, s) for s in spots]
    in_specs += [whole(w.shape) for w in weights] + [whole((tokens, width))] * 2
    operands = [hidden[0][s[0]] for s in spots] + [hidden[1]] * count + list(weights) + list(cot)
    aliases = {}
    if not first:
        in_specs += [whole((tokens, width))] * 2 + [anywhere]
        operands += list(state)
        aliases = {len(operands): 2}
    return pl.pallas_call(
        functools.partial(use_kernel, spots, len(weights), first),
        out_shape=[
            jax.ShapeDtypeStruct((tokens, width), F32),
            jax.ShapeDtypeStruct((tokens, width), F32),
            jax.ShapeDtypeStruct(hidden[1].shape, BF16),
            jax.ShapeDtypeStruct((tokens, count * 128), BF16),
        ],
        grid_spec=pltpu.PrefetchScalarGridSpec(
            num_scalar_prefetch=1,
            grid=(1,),
            in_specs=in_specs,
            out_specs=[whole((tokens, width))] * 2 + [anywhere, whole((tokens, count * 128))],
            scratch_shapes=[
                pltpu.VMEM((tokens, count * 128), BF16),
                pltpu.SemaphoreType.DMA((count,)),
            ],
        ),
        input_output_aliases=aliases,
        compiler_params=params(40),
        cost_estimate=COST if last else cost,
        name="use",
    )(place, *operands)


def merge_kernel(groups, place, *refs):
    parts, refs = refs[: len(groups)], refs[len(groups) :]
    own, other, _, keys, out, sems = refs
    copies = []
    for part, spots in zip(parts, groups):
        for k, (dx, dz, _) in enumerate(spots):
            at = pl.multiple_of(block_at(place, dx, dz, 1) * 128, 128)
            copies.append(
                pltpu.make_async_copy(
                    part.at[:, pl.ds(k * 128, 128)], out.at[:, pl.ds(at, 128)], sems.at[len(copies)]
                )
            )
            copies[-1].start()
    keys[...] = (own[...] + other[...]).astype(keys.dtype)
    for copy in copies:
        copy.wait()


def merge(place, parts, groups, keys, back):
    anywhere = pl.BlockSpec(memory_space=pl.ANY)
    shape = keys[0].shape
    return pl.pallas_call(
        functools.partial(merge_kernel, groups),
        out_shape=[jax.ShapeDtypeStruct(shape, BF16), jax.ShapeDtypeStruct(back.shape, back.dtype)],
        grid_spec=pltpu.PrefetchScalarGridSpec(
            num_scalar_prefetch=1,
            grid=(1,),
            in_specs=[whole(p.shape) for p in parts] + [whole(shape)] * 2 + [anywhere],
            out_specs=[whole(shape), anywhere],
            scratch_shapes=[pltpu.SemaphoreType.DMA((sum(map(len, groups)),))],
        ),
        input_output_aliases={len(parts) + 3: 1},
        compiler_params=params(24),
        cost_estimate=COST,
        name="merge",
    )(place, *parts, *keys, back)


def outer_update(global_rows, momentum_rows, outer_grad):
    new_momentum = 0.9 * momentum_rows + outer_grad
    new_global = global_rows - 0.7 * (outer_grad + 0.9 * new_momentum)
    return (new_global, new_momentum)


def local(hidden, kv_weight, kv_cotangent, outer_global, outer_local, outer_momentum):
    rows = hidden[0]
    cot = kv_cotangent[0]
    shard = kv_weight[0]
    scale = (rows.shape[0] * lax.axis_size("fsdp")) ** (-0.5)
    me = lax.axis_index("fsdp")
    place = jnp.stack([me // 16, (me // 2) % ZS, me % 2]).astype(jnp.int32)
    step = Order(place)
    replica_count = lax.axis_size("replica")

    def send(value, pairs):
        return lax.ppermute(step.gate(value), "fsdp", pairs)

    def butterfly(value, bit):
        pairs = [(r, r ^ bit) for r in range(replica_count)]
        return lax.ppermute(step.gate(value), "replica", pairs)

    def both_ways(above, below):
        above, below = step.wait(above.astype(F16), below.astype(F16))
        return send(above, Z_UP), send(below, Z_DOWN)

    b0 = send(shard, X_SWAP)
    other = send(rows, CORE_SWAP), send(cot, CORE_SWAP)
    total = outer_global - outer_local[0]
    summed = butterfly(total, 2)
    own = pack(rows, step.place)
    b0, summed, *both = step.wait(b0, summed, *other, *own)
    total = total + summed
    hidden2, cot2 = (both[2:], both[0]), (cot, both[1])
    pair = jnp.concatenate([shard, b0], axis=0)
    up1, down1 = send(pair, Z_UP), send(pair, Z_DOWN)
    summed = butterfly(total, 4)

    sizes = (384, 256, 256, 128)
    far = grad(step.place, 1, hidden2, cot2, sizes, scale * UP)
    far = step.wait(*[f.astype(F16) for f in far])
    got_a, got_b = send(far[0], X_SWAP), send(far[1], X_SWAP)
    near = step.wait(*grad(step.place, 0, hidden2, cot2, sizes, scale * UP))

    up1, down1, summed = step.wait(up1, down1, summed)
    total = total + summed
    up2, down2 = send(up1, Z_UP), send(down1, Z_DOWN)
    spots = [(0, 0, 0), (1, 0, 0), (0, -1, 0), (1, -1, 0), (0, 1, 0), (1, 1, 0)]
    groups = [spots]
    *state, back1 = step.wait(*use(step.place, hidden2, cot2, [pair, up1, down1], spots, None))

    def chip_sum(part, got, k):
        rows = slice(k * 128, (k + 1) * 128)
        return near[part][rows] + got[rows].astype(F32)

    (got_a,) = step.wait(got_a)
    above, below = chip_sum(0, got_a, 0), chip_sum(0, got_a, 1)
    above, below = send(above.astype(F16), Z_UP), send(below.astype(F16), Z_DOWN)
    up2, down2 = step.wait(up2, down2)
    up3, down3 = send(up2, Z_UP), send(down2, Z_DOWN)

    above, below, got = step.wait(above, below, got_b)
    above = chip_sum(1, got, 0) + above.astype(F32)
    below = chip_sum(1, got, 1) + below.astype(F32)
    above, below = send(above.astype(F16), Z_UP), send(below.astype(F16), Z_DOWN)
    got = send(far[2], X_SWAP)
    spots = [(0, -2, 0), (1, -2, 0), (0, 2, 0), (1, 2, 0)]
    groups.append(spots)
    *state, back2 = step.wait(*use(step.place, hidden2, cot2, [up2, down2], spots, state))
    back1 = jnp.concatenate([back1, back2], axis=1)
    (back1,) = step.wait(back1)

    up3, down3 = step.wait(up3, down3)
    up4, down4 = send(up3[:128], Z_UP), send(down3[128:], Z_DOWN)
    above, below, got = step.wait(above, below, got)
    above = send((chip_sum(2, got, 0) + above.astype(F32)).astype(F16), Z_UP)
    below = (chip_sum(2, got, 1) + below.astype(F32)).astype(F16)
    got = send(far[3], X_SWAP)
    summed = butterfly(total, 1)
    spots = [(0, -3, 0), (1, -3, 0), (0, 3, 0), (1, 3, 0)]
    groups.append(spots)
    *state, back3 = step.wait(*use(step.place, hidden2, cot2, [up3, down3], spots, state, True))
    up4, down4 = step.wait(up4, down4)
    spots = [(0, 4, 0), (1, 4, 0)]
    groups.append(spots)
    keys, other_keys, back, back4 = step.wait(*use(step.place, hidden2, cot2, [up4, down4], spots, state, True))

    above, got, summed = step.wait(above, got, summed)
    above = (chip_sum(3, got, 0) + above.astype(F32)).astype(F16)
    above, below = send(above, Z_UP), send(below, Z_DOWN)
    other_keys, back1 = send(other_keys, CORE_SWAP), send(back1, CORE_SWAP)
    back3 = send(jnp.concatenate([back3, back4], axis=1), CORE_SWAP)
    new_global, new_momentum = outer_update(outer_global, outer_momentum, (total + summed) / replica_count)
    other_keys, back1, back3, new_global, new_momentum = step.wait(
        other_keys, back1, back3, new_global, new_momentum
    )
    groups = [groups[0] + groups[1], groups[2] + groups[3]]
    keys, back = merge(step.place, [back1, back3], groups, (keys, other_keys), back)
    above, below, keys, back = step.wait(above, below, keys, back)
    mine = near[0][256:] + got_a[256:].astype(F32)
    grads = (mine + above.astype(F32) + below.astype(F32)) * (1.0 / UP)
    return (keys[None], back[None], grads[None], new_global, new_momentum)


def solution(mesh):
    return jax.shard_map(
        local,
        mesh=mesh,
        in_specs=(
            P("replica", "fsdp", None),
            P("replica", "fsdp", None),
            P("replica", "fsdp", None),
            P("fsdp", None),
            P("replica", "fsdp", None),
            P("fsdp", None),
        ),
        out_specs=(
            P("replica", "fsdp", None),
            P("replica", "fsdp", None),
            P("replica", "fsdp", None),
            P("fsdp", None),
            P("fsdp", None),
        ),
        check_vma=False,
    )
```

```python
import functools

import jax
import jax.numpy as jnp
from jax import lax
from jax.experimental import pallas as pl
from jax.experimental.pallas import tpu as pltpu
from jax.sharding import PartitionSpec as P

BF16, F16, F32 = jnp.bfloat16, jnp.float16, jnp.float32
ZS, CORES, XS = 8, 2, 2
UP = 8.0
ORDER = (4, -3, 0, 3, -2, 2, -1, 1)


def fsdp_perm(fn):
    pairs = []
    for x in range(XS):
        for z in range(ZS):
            for c in range(CORES):
                nx, nz, nc = fn(x, z, c)
                pairs.append((x * 16 + z * 2 + c, nx * 16 + (nz % ZS) * 2 + nc))
    return pairs


Z_UP = fsdp_perm(lambda x, z, c: (x, z + 1 - 2 * c, c))
Z_DOWN = fsdp_perm(lambda x, z, c: (x, z - 1 + 2 * c, c))
X_SWAP = fsdp_perm(lambda x, z, c: (1 - x, z, c))
CORE_SWAP = fsdp_perm(lambda x, z, c: (x, z, 1 - c))


class Order:
    def __init__(self, place):
        self.place = place

    def wait(self, *values):
        *values, self.place = lax.optimization_barrier((*values, self.place))
        return values

    def gate(self, value):
        return lax.optimization_barrier((value, self.place))[0]


def block_at(place, dx, dz, dc):
    core = (place[2] + dc) % CORES
    return ((place[0] + dx) % XS) * 16 + ((place[1] + (1 - 2 * core) * dz + ZS) % ZS) * 2 + core


def columns(tokens, spot):
    return pl.BlockSpec(
        (tokens, 128), lambda i, place: (0, block_at(place, *spot)), pipeline_mode=pl.Buffered(1)
    )


def packed(tokens, k):
    return pl.BlockSpec((tokens, 128), lambda i, place: (0, k), pipeline_mode=pl.Buffered(1))


def whole(shape):
    return pl.BlockSpec(shape, lambda i, place: (0, 0), pipeline_mode=pl.Buffered(1))


def params(mib):
    return pltpu.CompilerParams(vmem_limit_bytes=mib << 20)


COST = pl.CostEstimate(flops=1 << 20, bytes_accessed=1 << 16, transcendentals=0)


def pack_kernel(place, *refs):
    count = len(ORDER)
    for half, out in enumerate(refs[2 * count :]):
        for k in range(count):
            out[:, k * 128 : (k + 1) * 128] = refs[half * count + k][...]


def pack(hidden, place):
    tokens = hidden.shape[0]
    count = len(ORDER)
    spots = [(dx, dz, 0) for dx in (0, 1) for dz in ORDER]
    shape = (tokens, count * 128)
    return pl.pallas_call(
        pack_kernel,
        out_shape=[jax.ShapeDtypeStruct(shape, hidden.dtype)] * 2,
        grid_spec=pltpu.PrefetchScalarGridSpec(
            num_scalar_prefetch=1,
            grid=(1,),
            in_specs=[columns(tokens, s) for s in spots],
            out_specs=[whole(shape)] * 2,
        ),
        compiler_params=params(8),
        cost_estimate=COST,
        name="pack",
    )(place, *([hidden] * len(spots)))


def grad_kernel(sizes, scale, place, *refs):
    count = len(ORDER)
    own = refs[0][...]
    other = jnp.concatenate([r[...] for r in refs[1 : count + 1]], axis=1)
    own_cot, other_cot = refs[count + 1 : count + 3]
    outs = refs[count + 3 :]
    dims = (((0,), (0,)), ((), ()))
    width = own_cot.shape[1]
    step = 512
    for n in range(0, width, step):
        cols = slice(n, n + step)
        total = lax.dot_general(own, own_cot[:, cols], dims, preferred_element_type=F32)
        total += lax.dot_general(other, other_cot[:, cols], dims, preferred_element_type=F32)
        total = total * scale
        at = 0
        for out, size in zip(outs, sizes):
            out[:, cols] = total[at : at + size].astype(out.dtype)
            at += size


def grad(place, dx, hidden, cot, sizes, scale):
    tokens, width = cot[0].shape
    count = len(ORDER)
    spots = [(dx, dz, 0) for dz in ORDER]
    return pl.pallas_call(
        functools.partial(grad_kernel, sizes, scale),
        out_shape=[jax.ShapeDtypeStruct((s, width), F32) for s in sizes],
        grid_spec=pltpu.PrefetchScalarGridSpec(
            num_scalar_prefetch=1,
            grid=(1,),
            in_specs=[whole((tokens, count * 128))]
            + [columns(tokens, s) for s in spots]
            + [whole((tokens, width))] * 2,
            out_specs=[whole((s, width)) for s in sizes],
        ),
        compiler_params=params(24),
        cost_estimate=COST,
        name="grad",
    )(place, hidden[0][dx], *([hidden[1]] * count), *cot)


def use_kernel(spots, arrays, first, place, near, far, other, *refs):
    count = len(spots)
    weights, refs = refs[:arrays], refs[arrays:]
    cot, refs = refs[:2], refs[2:]
    if not first:
        acc, refs = refs[:2], refs[3:]
    out_keys, out_back, out_other, block, rows, sems = refs[:2], *refs[2:]
    places = [pl.ds(pl.multiple_of(block_at(place, *spot) * 128, 128), 128) for spot in spots]
    parts = [pl.ds(k * 128, 128) for k in range(count)]
    reads = [pltpu.make_async_copy(other.at[:, p], rows.at[:, q], sems.at[0, k]) for k, (p, q) in enumerate(zip(places, parts))]
    writes = [pltpu.make_async_copy(block.at[:, q], out_back.at[:, p], sems.at[1, k]) for k, (p, q) in enumerate(zip(places, parts))]
    for copy in reads:
        copy.start()
    weight = jnp.concatenate([r[...] for r in weights], axis=0)
    dims = (((1,), (1,)), ((), ()))
    block[...] = lax.dot_general(cot[0][...], weight, dims, preferred_element_type=F32).astype(BF16)
    for copy in writes:
        copy.start()
    out_other[...] = lax.dot_general(cot[1][...], weight, dims, preferred_element_type=F32).astype(BF16)
    sides = (near, far)
    own = [sides[dx][:, ORDER.index(dz) * 128 : ORDER.index(dz) * 128 + 128] for dx, dz, _ in spots]
    keys = jnp.dot(jnp.concatenate(own, axis=1), weight, preferred_element_type=F32)
    out_keys[0][...] = keys if first else keys + acc[0][...]
    for copy in reads:
        copy.wait()
    keys = jnp.dot(rows[...], weight, preferred_element_type=F32)
    out_keys[1][...] = keys if first else keys + acc[1][...]
    for copy in writes:
        copy.wait()


def use(place, hidden, cot, weights, spots, state, last=False):
    tokens, width = cot[0].shape
    count = len(spots)
    first = state is None
    flops = 8 * tokens * count * 128 * width
    cost = pl.CostEstimate(flops=flops, bytes_accessed=1 << 20, transcendentals=0)
    anywhere = pl.BlockSpec(memory_space=pl.ANY)
    vmem = pl.BlockSpec(memory_space=pltpu.VMEM)
    in_specs = [pl.BlockSpec(memory_space=pltpu.SMEM), vmem, vmem, anywhere] + [vmem] * (len(weights) + 2)
    operands = [place, *hidden[0], hidden[1], *weights, *cot]
    aliases = {}
    if not first:
        in_specs += [vmem, vmem, anywhere]
        operands += list(state)
        aliases = {len(operands) - 1: 2, len(operands) - 2: 1, len(operands) - 3: 0}
    return pl.pallas_call(
        functools.partial(use_kernel, spots, len(weights), first),
        out_shape=[
            jax.ShapeDtypeStruct((tokens, width), F32),
            jax.ShapeDtypeStruct((tokens, width), F32),
            jax.ShapeDtypeStruct(hidden[1].shape, BF16),
            jax.ShapeDtypeStruct((tokens, count * 128), BF16),
        ],
        in_specs=in_specs,
        out_specs=[vmem, vmem, anywhere, vmem],
        scratch_shapes=[
            pltpu.VMEM((tokens, count * 128), BF16),
            pltpu.VMEM((tokens, count * 128), BF16),
            pltpu.SemaphoreType.DMA((2, count)),
        ],
        input_output_aliases=aliases,
        compiler_params=params(40),
        cost_estimate=COST if last else cost,
        name="use",
    )(*operands)


def merge_kernel(groups, place, *refs):
    parts, refs = refs[: len(groups)], refs[len(groups) :]
    own, other, _, keys, out, sems = refs
    copies = []
    for part, spots in zip(parts, groups):
        for k, (dx, dz, _) in enumerate(spots):
            at = pl.multiple_of(block_at(place, dx, dz, 1) * 128, 128)
            copies.append(
                pltpu.make_async_copy(
                    part.at[:, pl.ds(k * 128, 128)], out.at[:, pl.ds(at, 128)], sems.at[len(copies)]
                )
            )
            copies[-1].start()
    keys[...] = (own[...] + other[...]).astype(keys.dtype)
    for copy in copies:
        copy.wait()


def merge(place, parts, groups, keys, back):
    anywhere = pl.BlockSpec(memory_space=pl.ANY)
    shape = keys[0].shape
    return pl.pallas_call(
        functools.partial(merge_kernel, groups),
        out_shape=[jax.ShapeDtypeStruct(shape, BF16), jax.ShapeDtypeStruct(back.shape, back.dtype)],
        grid_spec=pltpu.PrefetchScalarGridSpec(
            num_scalar_prefetch=1,
            grid=(1,),
            in_specs=[whole(p.shape) for p in parts] + [whole(shape)] * 2 + [anywhere],
            out_specs=[whole(shape), anywhere],
            scratch_shapes=[pltpu.SemaphoreType.DMA((sum(map(len, groups)),))],
        ),
        input_output_aliases={len(parts) + 3: 1},
        compiler_params=params(24),
        cost_estimate=COST,
        name="merge",
    )(place, *parts, *keys, back)


def outer_update(global_rows, momentum_rows, outer_grad):
    new_momentum = 0.9 * momentum_rows + outer_grad
    new_global = global_rows - 0.7 * (outer_grad + 0.9 * new_momentum)
    return (new_global, new_momentum)


def local(hidden, kv_weight, kv_cotangent, outer_global, outer_local, outer_momentum):
    rows = hidden[0]
    cot = kv_cotangent[0]
    shard = kv_weight[0]
    scale = (rows.shape[0] * lax.axis_size("fsdp")) ** (-0.5)
    me = lax.axis_index("fsdp")
    place = jnp.stack([me // 16, (me // 2) % ZS, me % 2]).astype(jnp.int32)
    step = Order(place)
    replica_count = lax.axis_size("replica")

    def send(value, pairs):
        return lax.ppermute(step.gate(value), "fsdp", pairs)

    def butterfly(value, bit):
        pairs = [(r, r ^ bit) for r in range(replica_count)]
        return lax.ppermute(step.gate(value), "replica", pairs)

    def both_ways(above, below):
        above, below = step.wait(above.astype(F16), below.astype(F16))
        return send(above, Z_UP), send(below, Z_DOWN)

    b0 = send(shard, X_SWAP)
    other = send(rows, CORE_SWAP), send(cot, CORE_SWAP)
    total = outer_global - outer_local[0]
    summed = butterfly(total, 2)
    own = pack(rows, step.place)
    b0, summed, *both = step.wait(b0, summed, *other, *own)
    total = total + summed
    hidden2, cot2 = (both[2:], both[0]), (cot, both[1])
    pair = jnp.concatenate([shard, b0], axis=0)
    up1, down1 = send(pair, Z_UP), send(pair, Z_DOWN)
    summed = butterfly(total, 4)

    sizes = (384, 256, 256, 128)
    far = grad(step.place, 1, hidden2, cot2, sizes, scale * UP)
    far = step.wait(*[f.astype(F16) for f in far])
    got_a, got_b = send(far[0], X_SWAP), send(far[1], X_SWAP)
    near = step.wait(*grad(step.place, 0, hidden2, cot2, sizes, scale * UP))

    up1, down1, summed = step.wait(up1, down1, summed)
    total = total + summed
    up2, down2 = send(up1, Z_UP), send(down1, Z_DOWN)
    spots = [(0, 0, 0), (1, 0, 0), (0, -1, 0), (1, -1, 0), (0, 1, 0), (1, 1, 0)]
    groups = [spots]
    *state, back1 = step.wait(*use(step.place, hidden2, cot2, [pair, up1, down1], spots, None))

    def chip_sum(part, got, k):
        rows = slice(k * 128, (k + 1) * 128)
        return near[part][rows] + got[rows].astype(F32)

    (got_a,) = step.wait(got_a)
    above, below = chip_sum(0, got_a, 0), chip_sum(0, got_a, 1)
    above, below = send(above.astype(F16), Z_UP), send(below.astype(F16), Z_DOWN)
    up2, down2 = step.wait(up2, down2)
    up3, down3 = send(up2, Z_UP), send(down2, Z_DOWN)

    above, below, got = step.wait(above, below, got_b)
    above = chip_sum(1, got, 0) + above.astype(F32)
    below = chip_sum(1, got, 1) + below.astype(F32)
    above, below = send(above.astype(F16), Z_UP), send(below.astype(F16), Z_DOWN)
    got = send(far[2], X_SWAP)
    spots = [(0, -2, 0), (1, -2, 0), (0, 2, 0), (1, 2, 0)]
    groups.append(spots)
    *state, back2 = step.wait(*use(step.place, hidden2, cot2, [up2, down2], spots, state))
    back1 = jnp.concatenate([back1, back2], axis=1)
    (back1,) = step.wait(back1)

    up3, down3 = step.wait(up3, down3)
    up4, down4 = send(up3[:128], Z_UP), send(down3[128:], Z_DOWN)
    above, below, got = step.wait(above, below, got)
    above = send((chip_sum(2, got, 0) + above.astype(F32)).astype(F16), Z_UP)
    below = (chip_sum(2, got, 1) + below.astype(F32)).astype(F16)
    got = send(far[3], X_SWAP)
    summed = butterfly(total, 1)
    spots = [(0, -3, 0), (1, -3, 0), (0, 3, 0), (1, 3, 0)]
    groups.append(spots)
    *state, back3 = step.wait(*use(step.place, hidden2, cot2, [up3, down3], spots, state, True))
    up4, down4 = step.wait(up4, down4)
    spots = [(0, 4, 0), (1, 4, 0)]
    groups.append(spots)
    keys, other_keys, back, back4 = step.wait(*use(step.place, hidden2, cot2, [up4, down4], spots, state, True))

    above, got, summed = step.wait(above, got, summed)
    above = (chip_sum(3, got, 0) + above.astype(F32)).astype(F16)
    above, below = send(above, Z_UP), send(below, Z_DOWN)
    other_keys, back1 = send(other_keys, CORE_SWAP), send(back1, CORE_SWAP)
    back3 = send(jnp.concatenate([back3, back4], axis=1), CORE_SWAP)
    new_global, new_momentum = outer_update(outer_global, outer_momentum, (total + summed) / replica_count)
    other_keys, back1, back3, new_global, new_momentum = step.wait(
        other_keys, back1, back3, new_global, new_momentum
    )
    groups = [groups[0] + groups[1], groups[2] + groups[3]]
    keys, back = merge(step.place, [back1, back3], groups, (keys, other_keys), back)
    above, below, keys, back = step.wait(above, below, keys, back)
    mine = near[0][256:] + got_a[256:].astype(F32)
    grads = (mine + above.astype(F32) + below.astype(F32)) * (1.0 / UP)
    return (keys[None], back[None], grads[None], new_global, new_momentum)


def solution(mesh):
    return jax.shard_map(
        local,
        mesh=mesh,
        in_specs=(
            P("replica", "fsdp", None),
            P("replica", "fsdp", None),
            P("replica", "fsdp", None),
            P("fsdp", None),
            P("replica", "fsdp", None),
            P("fsdp", None),
        ),
        out_specs=(
            P("replica", "fsdp", None),
            P("replica", "fsdp", None),
            P("replica", "fsdp", None),
            P("fsdp", None),
            P("fsdp", None),
        ),
        check_vma=False,
    )
```

```python
import functools

import jax
import jax.numpy as jnp
from jax import lax
from jax.experimental import pallas as pl
from jax.experimental.pallas import tpu as pltpu
from jax.sharding import PartitionSpec as P

BF16, F16, F32 = jnp.bfloat16, jnp.float16, jnp.float32
ZS, CORES, XS = 8, 2, 2
UP = 8.0
ORDER = (4, -3, 0, 3, -2, 2, -1, 1)


def fsdp_perm(fn):
    pairs = []
    for x in range(XS):
        for z in range(ZS):
            for c in range(CORES):
                nx, nz, nc = fn(x, z, c)
                pairs.append((x * 16 + z * 2 + c, nx * 16 + (nz % ZS) * 2 + nc))
    return pairs


Z_UP = fsdp_perm(lambda x, z, c: (x, z + 1 - 2 * c, c))
Z_DOWN = fsdp_perm(lambda x, z, c: (x, z - 1 + 2 * c, c))
X_SWAP = fsdp_perm(lambda x, z, c: (1 - x, z, c))
CORE_SWAP = fsdp_perm(lambda x, z, c: (x, z, 1 - c))


class Order:
    def __init__(self, place):
        self.place = place

    def wait(self, *values):
        *values, self.place = lax.optimization_barrier((*values, self.place))
        return values

    def gate(self, value):
        return lax.optimization_barrier((value, self.place))[0]


def block_at(place, dx, dz, dc):
    core = (place[2] + dc) % CORES
    return ((place[0] + dx) % XS) * 16 + ((place[1] + (1 - 2 * core) * dz + ZS) % ZS) * 2 + core


def columns(tokens, spot):
    return pl.BlockSpec(
        (tokens, 128), lambda i, place: (0, block_at(place, *spot)), pipeline_mode=pl.Buffered(1)
    )


def packed(tokens, k):
    return pl.BlockSpec((tokens, 128), lambda i, place: (0, k), pipeline_mode=pl.Buffered(1))


def whole(shape):
    return pl.BlockSpec(shape, lambda i, place: (0, 0), pipeline_mode=pl.Buffered(1))


def params(mib):
    return pltpu.CompilerParams(vmem_limit_bytes=mib << 20)


COST = pl.CostEstimate(flops=1 << 20, bytes_accessed=1 << 16, transcendentals=0)


def pack_kernel(place, *refs):
    count = len(ORDER)
    for half, out in enumerate(refs[2 * count :]):
        for k in range(count):
            out[:, k * 128 : (k + 1) * 128] = refs[half * count + k][...]


def pack(hidden, place):
    tokens = hidden.shape[0]
    count = len(ORDER)
    spots = [(dx, dz, 0) for dx in (0, 1) for dz in ORDER]
    shape = (tokens, count * 128)
    return pl.pallas_call(
        pack_kernel,
        out_shape=[jax.ShapeDtypeStruct(shape, hidden.dtype)] * 2,
        grid_spec=pltpu.PrefetchScalarGridSpec(
            num_scalar_prefetch=1,
            grid=(1,),
            in_specs=[columns(tokens, s) for s in spots],
            out_specs=[whole(shape)] * 2,
        ),
        compiler_params=params(8),
        cost_estimate=COST,
        name="pack",
    )(place, *([hidden] * len(spots)))


def grad_kernel(sizes, scale, place, *refs):
    count = len(ORDER)
    own = refs[0][...]
    other = jnp.concatenate([r[...] for r in refs[1 : count + 1]], axis=1)
    own_cot, other_cot = refs[count + 1 : count + 3]
    outs = refs[count + 3 :]
    dims = (((0,), (0,)), ((), ()))
    width = own_cot.shape[1]
    step = 512
    for n in range(0, width, step):
        cols = slice(n, n + step)
        total = lax.dot_general(own, own_cot[:, cols], dims, preferred_element_type=F32)
        total += lax.dot_general(other, other_cot[:, cols], dims, preferred_element_type=F32)
        total = total * scale
        at = 0
        for out, size in zip(outs, sizes):
            out[:, cols] = total[at : at + size].astype(out.dtype)
            at += size


def grad(place, dx, hidden, cot, sizes, scale):
    tokens, width = cot[0].shape
    count = len(ORDER)
    spots = [(dx, dz, 0) for dz in ORDER]
    return pl.pallas_call(
        functools.partial(grad_kernel, sizes, scale),
        out_shape=[jax.ShapeDtypeStruct((s, width), F32) for s in sizes],
        grid_spec=pltpu.PrefetchScalarGridSpec(
            num_scalar_prefetch=1,
            grid=(1,),
            in_specs=[whole((tokens, count * 128))]
            + [columns(tokens, s) for s in spots]
            + [whole((tokens, width))] * 2,
            out_specs=[whole((s, width)) for s in sizes],
        ),
        compiler_params=params(24),
        cost_estimate=COST,
        name="grad",
    )(place, hidden[0][dx], *([hidden[1]] * count), *cot)


def use_kernel(spots, arrays, first, before, place, near, far, other, *refs):
    count = len(spots)
    if before:
        earlier, refs = refs[0], refs[1:]
    weights, refs = refs[:arrays], refs[arrays:]
    cot, refs = refs[:2], refs[2:]
    if not first:
        acc, refs = refs[:2], refs[3:]
    out_keys, out_back, out_other, block, rows, sems = refs[:2], *refs[2:]
    places = [pl.ds(pl.multiple_of(block_at(place, *spot) * 128, 128), 128) for spot in spots]
    parts = [pl.ds(k * 128, 128) for k in range(count)]
    reads = [pltpu.make_async_copy(other.at[:, p], rows.at[:, q], sems.at[0, k]) for k, (p, q) in enumerate(zip(places, parts))]
    writes = [pltpu.make_async_copy(block.at[:, q], out_back.at[:, p], sems.at[1, k]) for k, (p, q) in enumerate(zip(places, parts))]
    for copy in reads:
        copy.start()
    weight = jnp.concatenate([r[...] for r in weights], axis=0)
    dims = (((1,), (1,)), ((), ()))
    block[...] = lax.dot_general(cot[0][...], weight, dims, preferred_element_type=F32).astype(BF16)
    for copy in writes:
        copy.start()
    if before:
        out_other[:, :before] = earlier[...]
    out_other[:, before:] = lax.dot_general(
        cot[1][...], weight, dims, preferred_element_type=F32
    ).astype(BF16)
    sides = (near, far)
    own = [sides[dx][:, ORDER.index(dz) * 128 : ORDER.index(dz) * 128 + 128] for dx, dz, _ in spots]
    keys = jnp.dot(jnp.concatenate(own, axis=1), weight, preferred_element_type=F32)
    out_keys[0][...] = keys if first else keys + acc[0][...]
    for copy in reads:
        copy.wait()
    keys = jnp.dot(rows[...], weight, preferred_element_type=F32)
    out_keys[1][...] = keys if first else keys + acc[1][...]
    for copy in writes:
        copy.wait()


def use(place, hidden, cot, weights, spots, state, last=False, earlier=None):
    tokens, width = cot[0].shape
    count = len(spots)
    first = state is None
    flops = 8 * tokens * count * 128 * width
    cost = pl.CostEstimate(flops=flops, bytes_accessed=1 << 20, transcendentals=0)
    anywhere = pl.BlockSpec(memory_space=pl.ANY)
    vmem = pl.BlockSpec(memory_space=pltpu.VMEM)
    extra = [] if earlier is None else [earlier]
    before = sum(e.shape[1] for e in extra)
    in_specs = [pl.BlockSpec(memory_space=pltpu.SMEM), vmem, vmem, anywhere]
    in_specs += [vmem] * (len(extra) + len(weights) + 2)
    operands = [place, *hidden[0], hidden[1], *extra, *weights, *cot]
    aliases = {}
    if not first:
        in_specs += [vmem, vmem, anywhere]
        operands += list(state)
        aliases = {len(operands) - 1: 2, len(operands) - 2: 1, len(operands) - 3: 0}
    return pl.pallas_call(
        functools.partial(use_kernel, spots, len(weights), first, before),
        out_shape=[
            jax.ShapeDtypeStruct((tokens, width), F32),
            jax.ShapeDtypeStruct((tokens, width), F32),
            jax.ShapeDtypeStruct(hidden[1].shape, BF16),
            jax.ShapeDtypeStruct((tokens, before + count * 128), BF16),
        ],
        in_specs=in_specs,
        out_specs=[vmem, vmem, anywhere, vmem],
        scratch_shapes=[
            pltpu.VMEM((tokens, count * 128), BF16),
            pltpu.VMEM((tokens, count * 128), BF16),
            pltpu.SemaphoreType.DMA((2, count)),
        ],
        input_output_aliases=aliases,
        compiler_params=params(40),
        cost_estimate=COST if last else cost,
        name="use",
    )(*operands)


def merge_kernel(groups, place, *refs):
    parts, refs = refs[: len(groups)], refs[len(groups) :]
    own, other, _, keys, out, sems = refs
    copies = []
    for part, spots in zip(parts, groups):
        for k, (dx, dz, _) in enumerate(spots):
            at = pl.multiple_of(block_at(place, dx, dz, 1) * 128, 128)
            copies.append(
                pltpu.make_async_copy(
                    part.at[:, pl.ds(k * 128, 128)], out.at[:, pl.ds(at, 128)], sems.at[len(copies)]
                )
            )
            copies[-1].start()
    keys[...] = (own[...] + other[...]).astype(keys.dtype)
    for copy in copies:
        copy.wait()


def merge(place, parts, groups, keys, back):
    anywhere = pl.BlockSpec(memory_space=pl.ANY)
    shape = keys[0].shape
    return pl.pallas_call(
        functools.partial(merge_kernel, groups),
        out_shape=[jax.ShapeDtypeStruct(shape, BF16), jax.ShapeDtypeStruct(back.shape, back.dtype)],
        grid_spec=pltpu.PrefetchScalarGridSpec(
            num_scalar_prefetch=1,
            grid=(1,),
            in_specs=[whole(p.shape) for p in parts] + [whole(shape)] * 2 + [anywhere],
            out_specs=[whole(shape), anywhere],
            scratch_shapes=[pltpu.SemaphoreType.DMA((sum(map(len, groups)),))],
        ),
        input_output_aliases={len(parts) + 3: 1},
        compiler_params=params(24),
        cost_estimate=COST,
        name="merge",
    )(place, *parts, *keys, back)


def outer_update(global_rows, momentum_rows, outer_grad):
    new_momentum = 0.9 * momentum_rows + outer_grad
    new_global = global_rows - 0.7 * (outer_grad + 0.9 * new_momentum)
    return (new_global, new_momentum)


def local(hidden, kv_weight, kv_cotangent, outer_global, outer_local, outer_momentum):
    rows = hidden[0]
    cot = kv_cotangent[0]
    shard = kv_weight[0]
    scale = (rows.shape[0] * lax.axis_size("fsdp")) ** (-0.5)
    me = lax.axis_index("fsdp")
    place = jnp.stack([me // 16, (me // 2) % ZS, me % 2]).astype(jnp.int32)
    step = Order(place)
    replica_count = lax.axis_size("replica")

    def send(value, pairs):
        return lax.ppermute(step.gate(value), "fsdp", pairs)

    def butterfly(value, bit):
        pairs = [(r, r ^ bit) for r in range(replica_count)]
        return lax.ppermute(step.gate(value), "replica", pairs)

    def both_ways(above, below):
        above, below = step.wait(above.astype(F16), below.astype(F16))
        return send(above, Z_UP), send(below, Z_DOWN)

    b0 = send(shard, X_SWAP)
    other = send(rows, CORE_SWAP), send(cot, CORE_SWAP)
    total = outer_global - outer_local[0]
    summed = butterfly(total, 2)
    own = pack(rows, step.place)
    b0, summed, *both = step.wait(b0, summed, *other, *own)
    total = total + summed
    hidden2, cot2 = (both[2:], both[0]), (cot, both[1])
    pair = jnp.concatenate([shard, b0], axis=0)
    up1, down1 = send(pair, Z_UP), send(pair, Z_DOWN)
    summed = butterfly(total, 4)

    sizes = (384, 256, 256, 128)
    far = grad(step.place, 1, hidden2, cot2, sizes, scale * UP)
    far = step.wait(*[f.astype(F16) for f in far])
    got_a, got_b = send(far[0], X_SWAP), send(far[1], X_SWAP)
    near = step.wait(*grad(step.place, 0, hidden2, cot2, sizes, scale * UP))

    up1, down1, summed = step.wait(up1, down1, summed)
    total = total + summed
    up2, down2 = send(up1, Z_UP), send(down1, Z_DOWN)
    spots = [(0, 0, 0), (1, 0, 0), (0, -1, 0), (1, -1, 0), (0, 1, 0), (1, 1, 0)]
    groups = [spots]
    *state, back1 = step.wait(*use(step.place, hidden2, cot2, [pair, up1, down1], spots, None))

    def chip_sum(part, got, k):
        rows = slice(k * 128, (k + 1) * 128)
        return near[part][rows] + got[rows].astype(F32)

    (got_a,) = step.wait(got_a)
    above, below = chip_sum(0, got_a, 0), chip_sum(0, got_a, 1)
    above, below = send(above.astype(F16), Z_UP), send(below.astype(F16), Z_DOWN)
    up2, down2 = step.wait(up2, down2)
    up3, down3 = send(up2, Z_UP), send(down2, Z_DOWN)

    above, below, got = step.wait(above, below, got_b)
    above = chip_sum(1, got, 0) + above.astype(F32)
    below = chip_sum(1, got, 1) + below.astype(F32)
    above, below = send(above.astype(F16), Z_UP), send(below.astype(F16), Z_DOWN)
    got = send(far[2], X_SWAP)
    spots = [(0, -2, 0), (1, -2, 0), (0, 2, 0), (1, 2, 0)]
    groups.append(spots)
    *state, back2 = step.wait(*use(step.place, hidden2, cot2, [up2, down2], spots, state))
    back1 = jnp.concatenate([back1, back2], axis=1)
    (back1,) = step.wait(back1)

    up3, down3 = step.wait(up3, down3)
    up4, down4 = send(up3[:128], Z_UP), send(down3[128:], Z_DOWN)
    above, below, got = step.wait(above, below, got)
    above = send((chip_sum(2, got, 0) + above.astype(F32)).astype(F16), Z_UP)
    below = (chip_sum(2, got, 1) + below.astype(F32)).astype(F16)
    got = send(far[3], X_SWAP)
    summed = butterfly(total, 1)
    spots = [(0, -3, 0), (1, -3, 0), (0, 3, 0), (1, 3, 0)]
    groups.append(spots)
    *state, back3 = step.wait(*use(step.place, hidden2, cot2, [up3, down3], spots, state, True))
    up4, down4 = step.wait(up4, down4)
    spots = [(0, 4, 0), (1, 4, 0)]
    groups.append(spots)
    keys, other_keys, back, back3 = step.wait(
        *use(step.place, hidden2, cot2, [up4, down4], spots, state, True, back3)
    )

    above, got, summed = step.wait(above, got, summed)
    above = (chip_sum(3, got, 0) + above.astype(F32)).astype(F16)
    above, below = send(above, Z_UP), send(below, Z_DOWN)
    other_keys, back1 = send(other_keys, CORE_SWAP), send(back1, CORE_SWAP)
    back3 = send(back3, CORE_SWAP)
    new_global, new_momentum = outer_update(outer_global, outer_momentum, (total + summed) / replica_count)
    other_keys, back1, back3, new_global, new_momentum = step.wait(
        other_keys, back1, back3, new_global, new_momentum
    )
    groups = [groups[0] + groups[1], groups[2] + groups[3]]
    keys, back = merge(step.place, [back1, back3], groups, (keys, other_keys), back)
    above, below, keys, back = step.wait(above, below, keys, back)
    mine = near[0][256:] + got_a[256:].astype(F32)
    grads = (mine + above.astype(F32) + below.astype(F32)) * (1.0 / UP)
    return (keys[None], back[None], grads[None], new_global, new_momentum)


def solution(mesh):
    return jax.shard_map(
        local,
        mesh=mesh,
        in_specs=(
            P("replica", "fsdp", None),
            P("replica", "fsdp", None),
            P("replica", "fsdp", None),
            P("fsdp", None),
            P("replica", "fsdp", None),
            P("fsdp", None),
        ),
        out_specs=(
            P("replica", "fsdp", None),
            P("replica", "fsdp", None),
            P("replica", "fsdp", None),
            P("fsdp", None),
            P("fsdp", None),
        ),
        check_vma=False,
    )
```
